32 devices in a mesh: dp: 4 (over x, core), seq: 8 (over z, y).
Axes of the slice: x: 2, y: 2, z: 4, core: 2. Of those that a mesh axis runs over, the one named last changes fastest.
Arguments:
- queries: bfloat16 [4, 1024, 4096], P('dp', 'seq'), may hold values from -2 to 2
- key_rows: bfloat16 [4, 1024, 4096], P('dp', 'seq'), may hold values from -2 to 2
- value_rows: bfloat16 [4, 1024, 4096], P('dp', 'seq'), may hold values from -6 to 6
- decay_rates: float32 [32], replicated, may hold values from 0 to 1, as said below
- norm_gain: float32 [4096], replicated, may hold values from 0.5 to 2
- reward_probe: float32 [4096], replicated, may hold values from -0.25 to 0.25
- step_ends: int32 [4, 64], P('dp'), may hold values from 0 to 1023, as said below
- step_counts: int32 [4, 64], P('dp'), may hold values from 0 to 8
Outputs:
- loss_total: float32 [], replicated
- grad_queries: bfloat16 [4, 1024, 4096], P('dp', 'seq')
- grad_keys: bfloat16 [4, 1024, 4096], P('dp', 'seq')
- grad_values: bfloat16 [4, 1024, 4096], P('dp', 'seq')
- grad_gain: float32 [4096], replicated
- grad_probe: float32 [4096], replicated
The draws below stay inside these ranges and needn't reach their ends.
Inputs may be any that keep to these rules, and one draw needn't show every extreme that they name: `decay_rates`: positive rates. `step_ends`: within a pack the positions strictly increase, and the last one is 1023.
All inputs are finite; a program needn't handle non-finite values.
Results may differ from the reference program's by a relative error of at most 0.0094.
Values sent between devices are 32-bit elements; how exact they have to be, the bound alone decides.
A program may use at most 192 MiB of HBM per device.

```python
import math
import jax
import jax.numpy as jnp
from jax import lax

HEADS = 32
HEAD_DIM = 128
FEATURES = 4096
SPAN = 128
LENGTH = 1024
PACKS = 4
STEPS = 64
ROLLOUTS = 8
N_SEQ = 8


def draw_decay_rates(key, part):
    key = jax.random.fold_in(key, 11)
    order_key, slow_key, fast_key = jax.random.split(key, 3)
    order = jax.random.permutation(order_key, HEADS)
    kept = HEADS // 2
    slow_pick = order < kept
    slow_rate = jnp.exp(jax.random.uniform(slow_key, (HEADS,), jnp.float32, math.log(0.1 / LENGTH), math.log(2.0 / LENGTH)))
    fast_rate = jnp.exp(jax.random.uniform(fast_key, (HEADS,), jnp.float32, math.log(4.0 / LENGTH), math.log(1.0 / 25.0)))
    return jnp.where(slow_pick, slow_rate, fast_rate)


def draw_step_ends(key, part):
    key = jax.random.fold_in(key, 23)
    pack_keys = jax.random.split(key, PACKS)

    def one_pack(pack_key):
        picks = jax.random.permutation(pack_key, LENGTH - 1)[:STEPS - 1].astype(jnp.int32)
        last_end = jnp.full((1,), LENGTH - 1, jnp.int32)
        return jnp.concatenate([jnp.sort(picks), last_end]).astype(jnp.int32)
    return jax.vmap(one_pack)(pack_keys)


def touch_ends(entries, stream_key, low, largest):
    index_at = [jax.random.randint(jax.random.fold_in(stream_key, axis), (), 0, length) for axis, length in enumerate(entries.shape)]
    main_axis = entries.shape.index(max(entries.shape))
    next_to = index_at[:main_axis] + [(index_at[main_axis] + 1) % entries.shape[main_axis]] + index_at[main_axis + 1:]
    return entries.at[tuple(index_at)].set(low).at[tuple(next_to)].set(largest)


def levels(rng, shape, cuts, least, largest):
    loudness = 1.0
    for axis_at, blocks in cuts:
        heights = jax.random.uniform(jax.random.fold_in(jax.random.fold_in(rng, 6), axis_at), (blocks,), jnp.float32, least / len(cuts), largest / len(cuts))
        loudness = loudness * jnp.repeat(jnp.exp(heights), shape[axis_at] // blocks).reshape((-1,) + (1,) * (len(shape) - 1 - axis_at))
    return loudness


def centred(rng, dims, scale, limit, shards=(), dtype=jnp.bfloat16):
    values = jax.random.normal(rng, dims, jnp.float32) * scale
    if len(shards) > 0:
        values = levels(rng, dims, shards, -0.22, 0.18) * values
    return jnp.clip(values, min=-limit, max=limit).astype(dtype)


def setup_inputs(seed: int = 0) -> dict:
    seeds = jax.random.split(jax.random.key(seed), 9)
    return {
        "queries": centred(seeds[0], (PACKS, LENGTH, FEATURES), 0.3, 2.0, ((0, 4), (1, 8))),
        "key_rows": centred(seeds[1], (PACKS, LENGTH, FEATURES), 0.3, 2.0, ((0, 4), (1, 8))),
        "value_rows": centred(seeds[2], (PACKS, LENGTH, FEATURES), 1.0, 6.0, ((0, 4), (1, 8))),
        "decay_rates": draw_decay_rates(jax.random.fold_in(seeds[8], 71), 0),
        "norm_gain": jnp.clip(jax.random.uniform(seeds[4], (FEATURES,), jnp.float32, 0.5, 2.0), 0.5, 2.0),
        "reward_probe": centred(seeds[5], (FEATURES,), (FEATURES // 8) ** -0.5, 0.25, (), jnp.float32),
        "step_ends": draw_step_ends(jax.random.fold_in(seeds[8], 71), 0),
        "step_counts": touch_ends(jax.random.randint(seeds[7], (PACKS, STEPS), 0, ROLLOUTS + 1), jax.random.fold_in(seeds[7], 1), 0, ROLLOUTS).astype(jnp.int32),
    }


loss_scaling = 32768.0
norm_epsilon = 1e-06
highest = lax.Precision.HIGHEST

def decay_tables(decay_rates, block_size):
    offsets = jnp.arange(block_size).astype(jnp.float32)
    gap = offsets[:, None] - offsets[None, :]
    causal = gap >= 0.0
    safe_gap = jnp.where(causal, gap, 0.0)
    within = jnp.where(causal[None], jnp.exp(-decay_rates[:, None, None] * safe_gap[None]), 0.0)
    rising = jnp.exp(-offsets[:, None] * decay_rates[None, :])
    falling = jnp.exp(-(block_size - offsets)[:, None] * decay_rates[None, :])
    return (within, rising, falling)

def wide(array):
    return array.astype(jnp.float32)

def state_of(key_block, value_block, falling):
    scaled_keys = (wide(key_block) * falling[:, :, None]).astype(jnp.bfloat16)
    return jnp.einsum('shd,she->hde', wide(scaled_keys), wide(value_block), precision=highest)

def reference(queries, key_rows, value_rows, decay_rates, norm_gain, reward_probe, step_ends, step_counts):
    within, rising, falling = decay_tables(decay_rates, SPAN)
    step_decay = jnp.exp(-decay_rates * SPAN)
    gain_heads = norm_gain.reshape(HEADS, HEAD_DIM)
    probe_heads = reward_probe.reshape(HEADS, HEAD_DIM)
    weights = gain_heads * probe_heads
    positions = jnp.arange(LENGTH).astype(jnp.int32)
    zero_state = jnp.zeros((HEADS, HEAD_DIM, HEAD_DIM), jnp.float32)

    def advance(carry, state):
        return (step_decay[:, None, None] * carry + state, carry)

    def front(pieces):
        query_block, key_block, value_block, prefix, targets = pieces
        scores = jnp.einsum('thd,shd->hts', wide(query_block), wide(key_block), precision=highest)
        mixing = (scores * within).astype(jnp.bfloat16)
        prefix_half = prefix.astype(jnp.bfloat16)
        inner_part = jnp.einsum('hts,she->the', wide(mixing), wide(value_block), precision=highest)
        outer_part = rising[:, :, None] * jnp.einsum('thd,hde->the', wide(query_block), wide(prefix_half), precision=highest)
        attended = inner_part + outer_part
        spread = jnp.sqrt(lax.optimization_barrier(jnp.mean(attended * attended, axis=-1, keepdims=True)) + norm_epsilon)
        normed = attended / spread
        logits = lax.optimization_barrier(jnp.sum(normed * weights[None], axis=(1, 2)))
        token_loss = jax.nn.softplus(logits) - targets * logits
        slope_term = loss_scaling * (jax.nn.sigmoid(logits) - targets) / LENGTH
        gain_part = lax.optimization_barrier(jnp.sum(slope_term[:, None, None] * normed * probe_heads[None], axis=0)).reshape(FEATURES)
        probe_part = lax.optimization_barrier(jnp.sum(slope_term[:, None, None] * normed * gain_heads[None], axis=0)).reshape(FEATURES)
        lifted = slope_term[:, None, None] * weights[None]
        out_grad = ((lifted - normed * lax.optimization_barrier(jnp.mean(lifted * normed, axis=-1, keepdims=True))) / spread).astype(jnp.bfloat16)
        scaled_queries = (wide(query_block) * rising[:, :, None]).astype(jnp.bfloat16)
        partial_state = jnp.einsum('thd,the->hde', wide(scaled_queries), wide(out_grad), precision=highest)
        return (jnp.sum(token_loss) / LENGTH, gain_part, probe_part, out_grad, partial_state)

    def back(pieces):
        query_block, key_block, value_block, out_grad, prefix, later = pieces
        scores = jnp.einsum('thd,shd->hts', wide(query_block), wide(key_block), precision=highest)
        mixing = (scores * within).astype(jnp.bfloat16)
        back_scores = jnp.einsum('the,she->hts', wide(out_grad), wide(value_block), precision=highest)
        back_mix = (back_scores * within).astype(jnp.bfloat16)
        prefix_half = wide(prefix.astype(jnp.bfloat16))
        later_half = wide(later.astype(jnp.bfloat16))
        grad_q = jnp.einsum('hts,shd->thd', wide(back_mix), wide(key_block), precision=highest)
        grad_q = grad_q + rising[:, :, None] * jnp.einsum('the,hde->thd', wide(out_grad), prefix_half, precision=highest)
        grad_k = jnp.einsum('hts,thd->shd', wide(back_mix), wide(query_block), precision=highest)
        grad_k = grad_k + falling[:, :, None] * jnp.einsum('she,hde->shd', wide(value_block), later_half, precision=highest)
        grad_v = jnp.einsum('hts,the->she', wide(mixing), wide(out_grad), precision=highest)
        grad_v = grad_v + falling[:, :, None] * jnp.einsum('shd,hde->she', wide(key_block), later_half, precision=highest)
        return (grad_q.astype(jnp.bfloat16), grad_k.astype(jnp.bfloat16), grad_v.astype(jnp.bfloat16))

    def one_pack(pack):
        query_pack, key_pack, value_pack, ends, counts = pack
        query_spans = query_pack.reshape(N_SEQ, SPAN, HEADS, HEAD_DIM)
        key_spans = key_pack.reshape(N_SEQ, SPAN, HEADS, HEAD_DIM)
        value_spans = value_pack.reshape(N_SEQ, SPAN, HEADS, HEAD_DIM)
        segment = lax.optimization_barrier(jnp.sum((ends[None, :] < positions[:, None]).astype(jnp.int32), axis=1))
        fractions = counts.astype(jnp.float32) / ROLLOUTS
        targets = jnp.take(fractions, segment).reshape(N_SEQ, SPAN)

        def state_pair(pair):
            return state_of(pair[0], pair[1], falling)
        states = lax.map(state_pair, (key_spans, value_spans))
        _, prefixes = lax.scan(advance, zero_state, states)
        losses, gains, probes, out_grads, partials = lax.map(front, (query_spans, key_spans, value_spans, prefixes, targets))
        _, laters = lax.scan(advance, zero_state, partials, reverse=True)
        grad_q, grad_k, grad_v = lax.map(back, (query_spans, key_spans, value_spans, out_grads, prefixes, laters))
        return (jnp.sum(losses), lax.optimization_barrier(jnp.sum(gains, axis=0)), lax.optimization_barrier(jnp.sum(probes, axis=0)), grad_q.reshape(LENGTH, FEATURES), grad_k.reshape(LENGTH, FEATURES), grad_v.reshape(LENGTH, FEATURES))
    results = lax.map(one_pack, (queries, key_rows, value_rows, step_ends, step_counts))
    loss_total = jnp.sum(results[0])
    grad_gain = lax.optimization_barrier(jnp.sum(results[1], axis=0))
    grad_probe = lax.optimization_barrier(jnp.sum(results[2], axis=0))
    return (loss_total, results[3], results[4], results[5], grad_gain, grad_probe)
```

```python
import functools

import jax
import jax.numpy as jnp
from jax import lax
from jax.experimental import pallas as pl
from jax.experimental.pallas import tpu as pltpu
from jax.sharding import PartitionSpec as P

ROLLOUTS = 8
CHUNK = 2
loss_scaling = 32768.0
norm_epsilon = 1e-06
MESH = pl.DeviceIdType.MESH
F32 = jnp.float32
BF16 = jnp.bfloat16


def dot(a, b, ca, cb):
    return lax.dot_general(a, b, (((ca,), (cb,)), ((), ())), preferred_element_type=F32)


def bits_of(count):
    steps = []
    bit = 1
    while bit < count:
        steps.append(bit)
        bit *= 2
    return steps


def layer(
    n_dp,
    n_seq,
    rates_ref,
    q_ref,
    k_ref,
    v_ref,
    gain_ref,
    probe_ref,
    ends_ref,
    counts_ref,
    loss_ref,
    gq_ref,
    gk_ref,
    gv_ref,
    ggain_ref,
    gprobe_ref,
    state,
    peer,
    cin,
    cout,
    give,
    take,
    bstate,
    bpeer,
    bcin,
    bcout,
    bgive,
    btake,
    prefix_half,
    mix,
    normed,
    slim,
    gk_part,
    gv_part,
    og,
    sq,
    logit_sum,
    sums,
    sums_in,
    send_a,
    recv_a,
    send_c,
    recv_c,
    send_p,
    recv_p,
    bsend_a,
    brecv_a,
    bsend_c,
    brecv_c,
    bsend_p,
    brecv_p,
    send_s,
    recv_s,
):
    heads = rates_ref.shape[0]
    span = q_ref.shape[0]
    width = q_ref.shape[1] // heads
    half = heads // 2
    chunks = half // CHUNK
    length = span * n_seq
    seq = lax.axis_index("seq")
    dp = lax.axis_index("dp")
    column = seq % 2
    group = seq // 2
    groups = n_seq // 2
    mate = seq + 1 - 2 * column
    own = column * half
    other = (1 - column) * half

    exchanges = []
    for bit in bits_of(n_dp):
        exchanges.append(("dp", dp + bit * (1 - 2 * ((dp // bit) % 2))))
    for bit in bits_of(n_seq):
        exchanges.append(("seq", seq + bit * (1 - 2 * ((seq // bit) % 2))))

    barrier = pltpu.get_barrier_semaphore()
    for axis, partner in exchanges:
        pl.semaphore_signal(barrier, inc=1, device_id={axis: partner}, device_id_type=MESH)

    @pl.when(group > 0)
    def _():
        pl.semaphore_signal(barrier, inc=1, device_id={"seq": seq - 2}, device_id_type=MESH)

    @pl.when(group < groups - 1)
    def _():
        pl.semaphore_signal(barrier, inc=1, device_id={"seq": seq + 2}, device_id_type=MESH)

    @pl.when(group == 0)
    def _():
        cin[...] = jnp.zeros_like(cin)

    @pl.when(group == groups - 1)
    def _():
        bcin[...] = jnp.zeros_like(bcin)

    logit_sum[...] = jnp.zeros_like(logit_sum)

    rows = lax.broadcasted_iota(jnp.int32, (span, width), 0).astype(F32)
    gap = (
        lax.broadcasted_iota(jnp.int32, (span, span), 0)
        - lax.broadcasted_iota(jnp.int32, (span, span), 1)
    ).astype(F32)
    causal = gap >= 0.0

    def cols(h):
        return pl.ds(pl.multiple_of(h * width, width), width)

    def within_of(h):
        return jnp.where(causal, jnp.exp(-rates_ref[h] * jnp.where(causal, gap, 0.0)), 0.0)

    def rising_of(h):
        return jnp.exp(-rates_ref[h] * rows)

    def falling_of(h):
        return jnp.exp(-rates_ref[h] * (span - rows))

    def copy(src, dst, send, recv, at, rel, j, target):
        return pltpu.make_async_remote_copy(
            src_ref=src.at[pl.ds(at, CHUNK)],
            dst_ref=dst.at[pl.ds(rel, CHUNK)],
            send_sem=send.at[j],
            recv_sem=recv.at[j],
            device_id={"seq": target},
            device_id_type=MESH,
        )

    def swap(j, back):
        if back:
            return copy(bstate, bpeer, bsend_a, brecv_a, other + j * CHUNK, j * CHUNK, j, mate)
        return copy(state, peer, send_a, recv_a, other + j * CHUNK, j * CHUNK, j, mate)

    def hop(j, back):
        if back:
            return copy(bcout, bcin, bsend_c, brecv_c, j * CHUNK, j * CHUNK, j, seq - 2)
        return copy(cout, cin, send_c, recv_c, j * CHUNK, j * CHUNK, j, seq + 2)

    def hand(j, back):
        if back:
            return copy(bgive, btake, bsend_p, brecv_p, j * CHUNK, j * CHUNK, j, mate)
        return copy(give, take, send_p, recv_p, j * CHUNK, j * CHUNK, j, mate)

    def chain(j, back):
        mine_ref, peer_ref, in_ref, out_ref, give_ref = (
            (bstate, bpeer, bcin, bcout, bgive) if back else (state, peer, cin, cout, give)
        )
        leads = (column == 1) if back else (column == 0)
        has_in = (group < groups - 1) if back else (group > 0)
        has_out = (group > 0) if back else (group < groups - 1)
        swap(j, back).wait_recv()

        @pl.when(has_in)
        def _():
            hop(j, back).wait_recv()

        kept = []
        for i in range(CHUNK):
            rel = j * CHUNK + i
            h = own + rel
            decay = jnp.exp(jnp.full((1, width), -rates_ref[h] * span, F32))
            one = jnp.ones_like(decay)
            zero = jnp.zeros_like(decay)
            lead_decay = jnp.where(leads, decay, one)
            trail_decay = jnp.where(leads, one, decay)
            mine = mine_ref[h]
            theirs = peer_ref[rel]
            carry = in_ref[rel]
            out_ref[rel] = decay * decay * carry + lead_decay * mine + trail_decay * theirs
            give_ref[rel] = lead_decay * carry + jnp.where(leads, one, zero) * mine
            kept.append(
                (trail_decay * carry + jnp.where(leads, zero, one) * theirs).astype(BF16)
            )

        @pl.when(has_out)
        def _():
            hop(j, back).start()

        hand(j, back).start()
        return kept

    def make_state(h):
        keys = (k_ref[:, cols(h)].astype(F32) * falling_of(h)).astype(BF16)
        state[h] = dot(keys, v_ref[:, cols(h)], 0, 0)

    def finish_front(h, inner, prefix):
        prefix_half[h] = prefix
        q = q_ref[:, cols(h)]
        attended = inner + rising_of(h) * dot(q, prefix, 1, 0)
        inverse = lax.rsqrt(jnp.mean(attended * attended, axis=1, keepdims=True) + norm_epsilon)
        unit = attended * inverse
        normed[h] = unit
        weights = gain_ref[pl.ds(h, 1), :] * probe_ref[pl.ds(h, 1), :]
        weighted = unit * weights
        slim[h] = (weights - unit * jnp.mean(weighted, axis=1, keepdims=True)) * inverse
        logit_sum[...] += weighted

    def inner_of(h):
        q = q_ref[:, cols(h)]
        mixed = (dot(q, k_ref[:, cols(h)], 1, 1) * within_of(h)).astype(BF16)
        mix[h] = mixed
        sq[h] = (q.astype(F32) * rising_of(h)).astype(BF16)
        return dot(mixed, v_ref[:, cols(h)], 1, 0)

    def make_first(j, carry):
        for i in range(CHUNK):
            make_state(other + j * CHUNK + i)
        return carry

    make_first(0, 0)
    edges = jnp.where(group > 0, 1, 0) + jnp.where(group < groups - 1, 1, 0)
    pl.semaphore_wait(barrier, len(exchanges) + edges)
    swap(0, False).start()

    def send_first(j, carry):
        make_first(j, carry)
        swap(j, False).start()
        return carry

    lax.fori_loop(1, chunks, send_first, 0)

    def forward(j, carry):
        for i in range(CHUNK):
            make_state(own + j * CHUNK + i)
        kept = chain(j, False)
        for i in range(CHUNK):
            h = own + j * CHUNK + i
            finish_front(h, inner_of(h), kept[i])
            h = other + j * CHUNK + i
            gk_part[h] = inner_of(h)
        return carry

    lax.fori_loop(0, chunks, forward, 0)

    def forward_rest(j, carry):
        hand(j, False).wait_recv()
        for i in range(CHUNK):
            rel = j * CHUNK + i
            h = other + rel
            finish_front(h, gk_part[h], take[rel].astype(BF16))
        return carry

    lax.fori_loop(0, chunks, forward_rest, 0)

    steps = ends_ref.shape[1]
    position = seq * span + lax.broadcasted_iota(jnp.int32, (span, steps), 0)
    segment = jnp.sum(jnp.where(ends_ref[...] < position, 1.0, 0.0), axis=1, keepdims=True)
    step_at = lax.broadcasted_iota(jnp.int32, (span, steps), 1).astype(F32)
    fractions = counts_ref[...].astype(F32) / ROLLOUTS
    targets = jnp.sum(jnp.where(step_at == segment, fractions, 0.0), axis=1, keepdims=True)
    logits = jnp.sum(logit_sum[...], axis=1, keepdims=True)
    soft = jnp.maximum(logits, 0.0) + jnp.log1p(jnp.exp(-jnp.abs(logits)))
    loss = jnp.sum(soft - targets * logits, axis=0, keepdims=True) / length
    slope = loss_scaling * (jax.nn.sigmoid(logits) - targets) / length
    slope_wide = jnp.broadcast_to(slope, (span, width))
    logit_sum[...] = slope_wide
    sums[0, pl.ds(heads, 8), :] = jnp.broadcast_to(loss, (8, width))

    def make_back(h):
        steep = logit_sum[...]
        grad = (steep * slim[h]).astype(BF16)
        og[h] = grad
        bstate[h] = dot(sq[h], grad, 0, 0)
        sums[0, pl.ds(h, 1), :] = jnp.sum(steep * normed[h], axis=0, keepdims=True)

    def send_back(j, carry):
        for i in range(CHUNK):
            make_back(other + j * CHUNK + i)
        swap(j, True).start()
        return carry

    lax.fori_loop(0, chunks, send_back, 0)

    def back_parts(h):
        grad = og[h]
        k = k_ref[:, cols(h)]
        q = q_ref[:, cols(h)]
        back_mix = (dot(grad, v_ref[:, cols(h)], 1, 1) * within_of(h)).astype(BF16)
        grad_q = dot(back_mix, k, 1, 0) + rising_of(h) * dot(grad, prefix_half[h], 1, 1)
        gq_ref[:, cols(h)] = grad_q.astype(BF16)
        return dot(back_mix, q, 0, 0), dot(mix[h], grad, 0, 0)

    def finish_back(h, grad_k, grad_v, later):
        falling = falling_of(h)
        grad_k = grad_k + falling * dot(v_ref[:, cols(h)], later, 1, 1)
        grad_v = grad_v + falling * dot(k_ref[:, cols(h)], later, 1, 0)
        gk_ref[:, cols(h)] = grad_k.astype(BF16)
        gv_ref[:, cols(h)] = grad_v.astype(BF16)

    def backward(j, carry):
        for i in range(CHUNK):
            make_back(own + j * CHUNK + i)
        kept = chain(j, True)
        for i in range(CHUNK):
            h = own + j * CHUNK + i
            grad_k, grad_v = back_parts(h)
            finish_back(h, grad_k, grad_v, kept[i])
            h = other + j * CHUNK + i
            gk_part[h], gv_part[h] = back_parts(h)
        return carry

    lax.fori_loop(0, chunks, backward, 0)

    def total(at):
        axis, partner = exchanges[at]
        return pltpu.make_async_remote_copy(
            src_ref=sums.at[at],
            dst_ref=sums_in.at[at],
            send_sem=send_s.at[at],
            recv_sem=recv_s.at[at],
            device_id={axis: partner},
            device_id_type=MESH,
        )

    def backward_rest(j):
        hand(j, True).wait_recv()
        for i in range(CHUNK):
            rel = j * CHUNK + i
            h = other + rel
            finish_back(h, gk_part[h], gv_part[h], btake[rel].astype(BF16))

    total(0).start()
    for j in range(max(chunks, len(exchanges))):
        if j < chunks:
            backward_rest(j)
        if j < len(exchanges):
            total(j).wait_recv()
            sums[j + 1] = sums[j] + sums_in[j]
            if j + 1 < len(exchanges):
                total(j + 1).start()

    last = len(exchanges)
    summed = sums[last, pl.ds(0, heads), :]
    ggain_ref[...] = summed * probe_ref[...]
    gprobe_ref[...] = summed * gain_ref[...]
    loss_ref[...] = sums[last, pl.ds(heads, 1), pl.ds(0, 1)]

    for at in range(len(exchanges)):
        total(at).wait_send()

    def drain(j, carry):
        for back in (False, True):
            swap(j, back).wait_send()
            hand(j, back).wait_send()

        @pl.when(group < groups - 1)
        def _():
            hop(j, False).wait_send()

        @pl.when(group > 0)
        def _():
            hop(j, True).wait_send()

        return carry

    lax.fori_loop(0, chunks, drain, 0)


def solution(mesh):
    n_dp = mesh.shape["dp"]
    n_seq = mesh.shape["seq"]
    exchanges = len(bits_of(n_dp)) + len(bits_of(n_seq))

    def on_device(
        queries, key_rows, value_rows, decay_rates, norm_gain, reward_probe, step_ends, step_counts
    ):
        heads = decay_rates.shape[0]
        _, span, features = queries.shape
        width = features // heads
        half = heads // 2
        chunks = half // CHUNK
        vmem = pl.BlockSpec(memory_space=pltpu.VMEM)
        rows = jax.ShapeDtypeStruct((span, features), BF16)
        table = jax.ShapeDtypeStruct((heads, width), F32)

        def scan_buffers():
            return [pltpu.VMEM((heads, width, width), F32)] + [
                pltpu.VMEM((half, width, width), F32)
            ] * 5

        loss, gq, gk, gv, ggain, gprobe = pl.pallas_call(
            functools.partial(layer, n_dp, n_seq),
            out_shape=(jax.ShapeDtypeStruct((1, 1), F32), rows, rows, rows, table, table),
            in_specs=[pl.BlockSpec(memory_space=pltpu.SMEM)] + [vmem] * 7,
            out_specs=(vmem,) * 6,
            scratch_shapes=scan_buffers()
            + scan_buffers()
            + [
                pltpu.VMEM((heads, width, width), BF16),
                pltpu.VMEM((heads, span, span), BF16),
                pltpu.VMEM((heads, span, width), F32),
                pltpu.VMEM((heads, span, width), F32),
                pltpu.VMEM((heads, span, width), F32),
                pltpu.VMEM((heads, span, width), F32),
                pltpu.VMEM((heads, span, width), BF16),
                pltpu.VMEM((heads, span, width), BF16),
                pltpu.VMEM((span, width), F32),
                pltpu.VMEM((exchanges + 1, heads + 8, width), F32),
                pltpu.VMEM((exchanges, heads + 8, width), F32),
            ]
            + [pltpu.SemaphoreType.DMA((chunks,))] * 12
            + [pltpu.SemaphoreType.DMA((exchanges,))] * 2,
            compiler_params=pltpu.CompilerParams(
                collective_id=0, has_side_effects=True, vmem_limit_bytes=48 * 1024 * 1024
            ),
            cost_estimate=pl.CostEstimate(
                flops=28 * heads * span * width * width,
                bytes_accessed=12 * span * features,
                transcendentals=6 * heads * span * width,
            ),
        )(
            decay_rates,
            queries[0],
            key_rows[0],
            value_rows[0],
            norm_gain.reshape(heads, width),
            reward_probe.reshape(heads, width),
            step_ends,
            step_counts,
        )
        return (
            loss.reshape(()),
            gq[None],
            gk[None],
            gv[None],
            ggain.reshape(features),
            gprobe.reshape(features),
        )

    rows = P("dp", "seq", None)
    return jax.shard_map(
        on_device,
        mesh=mesh,
        in_specs=(rows, rows, rows, P(), P(), P(), P("dp", None), P("dp", None)),
        out_specs=(P(), rows, rows, rows, P(), P()),
        check_vma=False,
    )
```

```python
import functools

import jax
import jax.numpy as jnp
from jax import lax
from jax.experimental import pallas as pl
from jax.experimental.pallas import tpu as pltpu
from jax.sharding import PartitionSpec as P

ROLLOUTS = 8
CHUNK = 2
FLIGHT = 2
loss_scaling = 32768.0
norm_epsilon = 1e-06
MESH = pl.DeviceIdType.MESH
F32 = jnp.float32
BF16 = jnp.bfloat16


def dot(a, b, ca, cb):
    return lax.dot_general(a, b, (((ca,), (cb,)), ((), ())), preferred_element_type=F32)


def bits_of(count):
    steps = []
    bit = 1
    while bit < count:
        steps.append(bit)
        bit *= 2
    return steps


def layer(
    n_dp,
    n_seq,
    rates_ref,
    q_ref,
    k_ref,
    v_ref,
    gain_ref,
    probe_ref,
    ends_ref,
    counts_ref,
    loss_ref,
    gq_ref,
    gk_ref,
    gv_ref,
    ggain_ref,
    gprobe_ref,
    state,
    peer,
    cin,
    cout,
    give,
    take,
    bstate,
    bpeer,
    bcin,
    bcout,
    bgive,
    btake,
    prefix_half,
    later_half,
    mix,
    normed,
    slim,
    gk_part,
    gv_part,
    og,
    sq,
    logit_sum,
    sums,
    sums_in,
    send_a,
    recv_a,
    send_c,
    recv_c,
    send_p,
    recv_p,
    bsend_a,
    brecv_a,
    bsend_c,
    brecv_c,
    bsend_p,
    brecv_p,
    send_s,
    recv_s,
):
    heads = rates_ref.shape[0]
    span = q_ref.shape[0]
    width = q_ref.shape[1] // heads
    half = heads // 2
    chunks = half // CHUNK
    length = span * n_seq
    seq = lax.axis_index("seq")
    dp = lax.axis_index("dp")
    column = seq % 2
    group = seq // 2
    groups = n_seq // 2
    mate = seq + 1 - 2 * column
    own = column * half
    other = (1 - column) * half

    exchanges = []
    for bit in bits_of(n_dp):
        exchanges.append(("dp", dp + bit * (1 - 2 * ((dp // bit) % 2))))
    for bit in bits_of(n_seq):
        exchanges.append(("seq", seq + bit * (1 - 2 * ((seq // bit) % 2))))

    barrier = pltpu.get_barrier_semaphore()
    for axis, partner in exchanges:
        pl.semaphore_signal(barrier, inc=1, device_id={axis: partner}, device_id_type=MESH)

    @pl.when(group > 0)
    def _():
        pl.semaphore_signal(barrier, inc=1, device_id={"seq": seq - 2}, device_id_type=MESH)

    @pl.when(group < groups - 1)
    def _():
        pl.semaphore_signal(barrier, inc=1, device_id={"seq": seq + 2}, device_id_type=MESH)

    @pl.when(group == 0)
    def _():
        cin[...] = jnp.zeros_like(cin)

    @pl.when(group == groups - 1)
    def _():
        bcin[...] = jnp.zeros_like(bcin)

    logit_sum[...] = jnp.zeros_like(logit_sum)

    rows = lax.broadcasted_iota(jnp.int32, (span, width), 0).astype(F32)
    gap = (
        lax.broadcasted_iota(jnp.int32, (span, span), 0)
        - lax.broadcasted_iota(jnp.int32, (span, span), 1)
    ).astype(F32)
    causal = gap >= 0.0

    def cols(h):
        return pl.ds(pl.multiple_of(h * width, width), width)

    def within_of(h):
        return jnp.where(causal, jnp.exp(-rates_ref[h] * jnp.where(causal, gap, 0.0)), 0.0)

    def rising_of(h):
        return jnp.exp(-rates_ref[h] * rows)

    def falling_of(h):
        return jnp.exp(-rates_ref[h] * (span - rows))

    def copy(src, dst, send, recv, at, rel, j, target):
        return pltpu.make_async_remote_copy(
            src_ref=src.at[pl.ds(at, CHUNK)],
            dst_ref=dst.at[pl.ds(rel, CHUNK)],
            send_sem=send.at[j],
            recv_sem=recv.at[j],
            device_id={"seq": target},
            device_id_type=MESH,
        )

    def swap(j, back):
        if back:
            return copy(bstate, bpeer, bsend_a, brecv_a, other + j * CHUNK, j * CHUNK, j, mate)
        return copy(state, peer, send_a, recv_a, other + j * CHUNK, j * CHUNK, j, mate)

    def hop(j, back):
        if back:
            return copy(bcout, bcin, bsend_c, brecv_c, j * CHUNK, j * CHUNK, j, seq - 2)
        return copy(cout, cin, send_c, recv_c, j * CHUNK, j * CHUNK, j, seq + 2)

    def hand(j, back):
        if back:
            return copy(bgive, btake, bsend_p, brecv_p, j * CHUNK, j * CHUNK, j, mate)
        return copy(give, take, send_p, recv_p, j * CHUNK, j * CHUNK, j, mate)

    def chain(j, back):
        mine_ref, peer_ref, in_ref, out_ref, give_ref = (
            (bstate, bpeer, bcin, bcout, bgive) if back else (state, peer, cin, cout, give)
        )
        leads = (column == 1) if back else (column == 0)
        has_in = (group < groups - 1) if back else (group > 0)
        has_out = (group > 0) if back else (group < groups - 1)

        @pl.when(has_in)
        def _():
            hop(j, back).wait_recv()

        for i in range(CHUNK):
            rel = j * CHUNK + i
            h = own + rel
            decay = jnp.exp(jnp.full((1, width), -rates_ref[h] * span, F32))
            one = jnp.ones_like(decay)
            zero = jnp.zeros_like(decay)
            lead_decay = jnp.where(leads, decay, one)
            trail_decay = jnp.where(leads, one, decay)
            mine = mine_ref[h]
            theirs = peer_ref[rel]
            carry = in_ref[rel]
            out_ref[rel] = decay * decay * carry + lead_decay * mine + trail_decay * theirs
            give_ref[rel] = lead_decay * carry + jnp.where(leads, one, zero) * mine
            kept = (trail_decay * carry + jnp.where(leads, zero, one) * theirs).astype(BF16)
            if back:
                later_half[rel] = kept
            else:
                prefix_half[h] = kept

        @pl.when(has_out)
        def _():
            hop(j, back).start()

    def make_state(h):
        keys = (k_ref[:, cols(h)].astype(F32) * falling_of(h)).astype(BF16)
        state[h] = dot(keys, v_ref[:, cols(h)], 0, 0)

    def finish_front(h, inner, prefix):
        q = q_ref[:, cols(h)]
        attended = inner + rising_of(h) * dot(q, prefix, 1, 0)
        inverse = lax.rsqrt(jnp.mean(attended * attended, axis=1, keepdims=True) + norm_epsilon)
        unit = attended * inverse
        normed[h] = unit
        weights = gain_ref[pl.ds(h, 1), :] * probe_ref[pl.ds(h, 1), :]
        weighted = unit * weights
        slim[h] = (weights - unit * jnp.mean(weighted, axis=1, keepdims=True)) * inverse
        logit_sum[...] += weighted

    def inner_of(h):
        q = q_ref[:, cols(h)]
        mixed = (dot(q, k_ref[:, cols(h)], 1, 1) * within_of(h)).astype(BF16)
        mix[h] = mixed
        sq[h] = (q.astype(F32) * rising_of(h)).astype(BF16)
        return dot(mixed, v_ref[:, cols(h)], 1, 0)

    def make_first(j, carry):
        for i in range(CHUNK):
            make_state(other + j * CHUNK + i)
        return carry

    flight = min(FLIGHT, chunks)

    def lead_first(j, carry):
        make_first(j, carry)
        swap(j, False).start()
        return carry

    make_first(0, 0)
    edges = jnp.where(group > 0, 1, 0) + jnp.where(group < groups - 1, 1, 0)
    pl.semaphore_wait(barrier, len(exchanges) + edges)
    swap(0, False).start()
    lax.fori_loop(1, flight, lead_first, 0)
    lax.fori_loop(flight, chunks, make_first, 0)

    def make_own(j):
        for i in range(CHUNK):
            make_state(own + j * CHUNK + i)

    make_own(0)

    steps = ends_ref.shape[1]
    position = seq * span + lax.broadcasted_iota(jnp.int32, (span, steps), 0)
    segment = jnp.sum(jnp.where(ends_ref[...] < position, 1.0, 0.0), axis=1, keepdims=True)
    step_at = lax.broadcasted_iota(jnp.int32, (span, steps), 1).astype(F32)
    fractions = counts_ref[...].astype(F32) / ROLLOUTS
    targets = jnp.sum(jnp.where(step_at == segment, fractions, 0.0), axis=1, keepdims=True)

    def pace(i, back, after):
        place = (groups - 1 - group) if back else group
        at = i - jnp.minimum(2 * place, chunks - flight)

        @pl.when((at >= 0) & (at < chunks))
        def _():
            chain(at, back)

        @pl.when(i + flight < chunks)
        def _():
            swap(i + flight, back).start()

        @pl.when((i + flight >= chunks) & (i + flight < 2 * chunks))
        def _():
            hand(i + flight - chunks, back).start()

        @pl.when((at >= 0) & (at < chunks))
        def _():
            after(at)

    def own_front(j):
        for i in range(CHUNK):
            h = own + j * CHUNK + i
            finish_front(h, inner_of(h), prefix_half[h])

    def forward(i, carry):
        swap(i, False).wait_recv()
        pace(i, False, own_front)

        @pl.when(i + 1 < chunks)
        def _():
            make_own(i + 1)

        for c in range(CHUNK):
            h = other + i * CHUNK + c
            gk_part[h] = inner_of(h)
        return carry

    lax.fori_loop(0, chunks, forward, 0)

    def forward_rest(j, carry):
        hand(j, False).wait_recv()
        pace(j + chunks, False, own_front)
        for i in range(CHUNK):
            rel = j * CHUNK + i
            h = other + rel
            prefix_half[h] = take[rel].astype(BF16)
            finish_front(h, gk_part[h], prefix_half[h])
        return carry

    lax.fori_loop(0, chunks, forward_rest, 0)

    logits = jnp.sum(logit_sum[...], axis=1, keepdims=True)
    soft = jnp.maximum(logits, 0.0) + jnp.log1p(jnp.exp(-jnp.abs(logits)))
    loss = jnp.sum(soft - targets * logits, axis=0, keepdims=True) / length
    slope = loss_scaling * (jax.nn.sigmoid(logits) - targets) / length
    slope_wide = jnp.broadcast_to(slope, (span, width))
    logit_sum[...] = slope_wide
    sums[0, pl.ds(heads, 8), :] = jnp.broadcast_to(loss, (8, width))

    def make_back(h):
        steep = logit_sum[...]
        grad = (steep * slim[h]).astype(BF16)
        og[h] = grad
        bstate[h] = dot(sq[h], grad, 0, 0)
        sums[0, pl.ds(h, 1), :] = jnp.sum(steep * normed[h], axis=0, keepdims=True)

    def back_first(j, carry):
        for i in range(CHUNK):
            make_back(other + j * CHUNK + i)
        return carry

    def lead_back(j, carry):
        back_first(j, carry)
        swap(j, True).start()
        return carry

    lax.fori_loop(0, flight, lead_back, 0)
    lax.fori_loop(flight, chunks, back_first, 0)

    def back_own(j):
        for i in range(CHUNK):
            make_back(own + j * CHUNK + i)

    back_own(0)

    def back_parts(h):
        grad = og[h]
        k = k_ref[:, cols(h)]
        q = q_ref[:, cols(h)]
        back_mix = (dot(grad, v_ref[:, cols(h)], 1, 1) * within_of(h)).astype(BF16)
        grad_q = dot(back_mix, k, 1, 0) + rising_of(h) * dot(grad, prefix_half[h], 1, 1)
        gq_ref[:, cols(h)] = grad_q.astype(BF16)
        return dot(back_mix, q, 0, 0), dot(mix[h], grad, 0, 0)

    def finish_back(h, grad_k, grad_v, later):
        falling = falling_of(h)
        grad_k = grad_k + falling * dot(v_ref[:, cols(h)], later, 1, 1)
        grad_v = grad_v + falling * dot(k_ref[:, cols(h)], later, 1, 0)
        gk_ref[:, cols(h)] = grad_k.astype(BF16)
        gv_ref[:, cols(h)] = grad_v.astype(BF16)

    def own_back(j):
        for i in range(CHUNK):
            h = own + j * CHUNK + i
            grad_k, grad_v = back_parts(h)
            finish_back(h, grad_k, grad_v, later_half[j * CHUNK + i])

    def backward(i, carry):
        swap(i, True).wait_recv()
        pace(i, True, own_back)

        @pl.when(i + 1 < chunks)
        def _():
            back_own(i + 1)

        for c in range(CHUNK):
            h = other + i * CHUNK + c
            gk_part[h], gv_part[h] = back_parts(h)
        return carry

    lax.fori_loop(0, chunks, backward, 0)

    def total(at):
        axis, partner = exchanges[at]
        return pltpu.make_async_remote_copy(
            src_ref=sums.at[at],
            dst_ref=sums_in.at[at],
            send_sem=send_s.at[at],
            recv_sem=recv_s.at[at],
            device_id={axis: partner},
            device_id_type=MESH,
        )

    def backward_rest(j):
        hand(j, True).wait_recv()
        pace(j + chunks, True, own_back)
        for i in range(CHUNK):
            rel = j * CHUNK + i
            h = other + rel
            finish_back(h, gk_part[h], gv_part[h], btake[rel].astype(BF16))

    total(0).start()
    for j in range(max(chunks, len(exchanges))):
        if j < chunks:
            backward_rest(j)
        if j < len(exchanges):
            total(j).wait_recv()
            sums[j + 1] = sums[j] + sums_in[j]
            if j + 1 < len(exchanges):
                total(j + 1).start()

    last = len(exchanges)
    summed = sums[last, pl.ds(0, heads), :]
    ggain_ref[...] = summed * probe_ref[...]
    gprobe_ref[...] = summed * gain_ref[...]
    loss_ref[...] = sums[last, pl.ds(heads, 1), pl.ds(0, 1)]

    for at in range(len(exchanges)):
        total(at).wait_send()

    def drain(j, carry):
        for back in (False, True):
            swap(j, back).wait_send()
            hand(j, back).wait_send()

        @pl.when(group < groups - 1)
        def _():
            hop(j, False).wait_send()

        @pl.when(group > 0)
        def _():
            hop(j, True).wait_send()

        return carry

    lax.fori_loop(0, chunks, drain, 0)


def solution(mesh):
    n_dp = mesh.shape["dp"]
    n_seq = mesh.shape["seq"]
    exchanges = len(bits_of(n_dp)) + len(bits_of(n_seq))

    def on_device(
        queries, key_rows, value_rows, decay_rates, norm_gain, reward_probe, step_ends, step_counts
    ):
        heads = decay_rates.shape[0]
        _, span, features = queries.shape
        width = features // heads
        half = heads // 2
        chunks = half // CHUNK
        vmem = pl.BlockSpec(memory_space=pltpu.VMEM)
        rows = jax.ShapeDtypeStruct((span, features), BF16)
        table = jax.ShapeDtypeStruct((heads, width), F32)

        def scan_buffers():
            return [pltpu.VMEM((heads, width, width), F32)] + [
                pltpu.VMEM((half, width, width), F32)
            ] * 5

        loss, gq, gk, gv, ggain, gprobe = pl.pallas_call(
            functools.partial(layer, n_dp, n_seq),
            out_shape=(jax.ShapeDtypeStruct((1, 1), F32), rows, rows, rows, table, table),
            in_specs=[pl.BlockSpec(memory_space=pltpu.SMEM)] + [vmem] * 7,
            out_specs=(vmem,) * 6,
            scratch_shapes=scan_buffers()
            + scan_buffers()
            + [
                pltpu.VMEM((heads, width, width), BF16),
                pltpu.VMEM((half, width, width), BF16),
                pltpu.VMEM((heads, span, span), BF16),
                pltpu.VMEM((heads, span, width), F32),
                pltpu.VMEM((heads, span, width), F32),
                pltpu.VMEM((heads, span, width), F32),
                pltpu.VMEM((heads, span, width), F32),
                pltpu.VMEM((heads, span, width), BF16),
                pltpu.VMEM((heads, span, width), BF16),
                pltpu.VMEM((span, width), F32),
                pltpu.VMEM((exchanges + 1, heads + 8, width), F32),
                pltpu.VMEM((exchanges, heads + 8, width), F32),
            ]
            + [pltpu.SemaphoreType.DMA((chunks,))] * 12
            + [pltpu.SemaphoreType.DMA((exchanges,))] * 2,
            compiler_params=pltpu.CompilerParams(
                collective_id=0, has_side_effects=True, vmem_limit_bytes=48 * 1024 * 1024
            ),
            cost_estimate=pl.CostEstimate(
                flops=28 * heads * span * width * width,
                bytes_accessed=12 * span * features,
                transcendentals=6 * heads * span * width,
            ),
        )(
            decay_rates,
            queries[0],
            key_rows[0],
            value_rows[0],
            norm_gain.reshape(heads, width),
            reward_probe.reshape(heads, width),
            step_ends,
            step_counts,
        )
        return (
            loss.reshape(()),
            gq[None],
            gk[None],
            gv[None],
            ggain.reshape(features),
            gprobe.reshape(features),
        )

    rows = P("dp", "seq", None)
    return jax.shard_map(
        on_device,
        mesh=mesh,
        in_specs=(rows, rows, rows, P(), P(), P(), P("dp", None), P("dp", None)),
        out_specs=(P(), rows, rows, rows, P(), P()),
        check_vma=False,
    )
```

```python
import functools

import jax
import jax.numpy as jnp
from jax import lax
from jax.experimental import pallas as pl
from jax.experimental.pallas import tpu as pltpu
from jax.sharding import PartitionSpec as P

ROLLOUTS = 8
CHUNK = 2
FLIGHT = 2
loss_scaling = 32768.0
norm_epsilon = 1e-06
MESH = pl.DeviceIdType.MESH
F32 = jnp.float32
BF16 = jnp.bfloat16


def dot(a, b, ca, cb):
    return lax.dot_general(a, b, (((ca,), (cb,)), ((), ())), preferred_element_type=F32)


def bits_of(count):
    steps = []
    bit = 1
    while bit < count:
        steps.append(bit)
        bit *= 2
    return steps


def layer(
    n_dp,
    n_seq,
    rates_hbm,
    q_hbm,
    k_hbm,
    v_hbm,
    gain_hbm,
    probe_hbm,
    ends_hbm,
    counts_hbm,
    loss_ref,
    gq_hbm,
    gk_hbm,
    gv_hbm,
    ggain_ref,
    gprobe_ref,
    gq_ref,
    gk_ref,
    gv_ref,
    save_sem,
    rates_ref,
    q_ref,
    k_ref,
    v_ref,
    gain_ref,
    probe_ref,
    ends_ref,
    counts_ref,
    load_sem,
    state,
    peer,
    cin,
    cout,
    give,
    take,
    bstate,
    bpeer,
    bcin,
    bcout,
    bgive,
    btake,
    prefix_half,
    later_half,
    mix,
    normed,
    slim,
    gk_part,
    gv_part,
    og,
    sq,
    logit_sum,
    sums,
    sums_in,
    send_a,
    recv_a,
    send_c,
    recv_c,
    send_p,
    recv_p,
    bsend_a,
    brecv_a,
    bsend_c,
    brecv_c,
    bsend_p,
    brecv_p,
    send_s,
    recv_s,
):
    loads = []
    for at, (source, target) in enumerate(
        (
            (rates_hbm, rates_ref),
            (k_hbm, k_ref),
            (v_hbm, v_ref),
            (ends_hbm, ends_ref),
            (counts_hbm, counts_ref),
            (gain_hbm, gain_ref),
            (probe_hbm, probe_ref),
            (q_hbm, q_ref),
        )
    ):
        loads.append(pltpu.make_async_copy(source, target, load_sem.at[at]))
        loads[-1].start()

    heads = rates_ref.shape[0]
    span = q_ref.shape[0]
    width = q_ref.shape[1] // heads
    half = heads // 2
    chunks = half // CHUNK
    length = span * n_seq
    seq = lax.axis_index("seq")
    dp = lax.axis_index("dp")
    column = seq % 2
    group = seq // 2
    groups = n_seq // 2
    mate = seq + 1 - 2 * column
    own = column * half
    other = (1 - column) * half

    exchanges = []
    for bit in bits_of(n_dp):
        exchanges.append(("dp", dp + bit * (1 - 2 * ((dp // bit) % 2))))
    for bit in bits_of(n_seq):
        exchanges.append(("seq", seq + bit * (1 - 2 * ((seq // bit) % 2))))

    barrier = pltpu.get_barrier_semaphore()
    for axis, partner in exchanges:
        pl.semaphore_signal(barrier, inc=1, device_id={axis: partner}, device_id_type=MESH)

    @pl.when(group > 0)
    def _():
        pl.semaphore_signal(barrier, inc=1, device_id={"seq": seq - 2}, device_id_type=MESH)

    @pl.when(group < groups - 1)
    def _():
        pl.semaphore_signal(barrier, inc=1, device_id={"seq": seq + 2}, device_id_type=MESH)

    @pl.when(group == 0)
    def _():
        cin[...] = jnp.zeros_like(cin)

    @pl.when(group == groups - 1)
    def _():
        bcin[...] = jnp.zeros_like(bcin)

    logit_sum[...] = jnp.zeros_like(logit_sum)

    rows = lax.broadcasted_iota(jnp.int32, (span, width), 0).astype(F32)
    gap = (
        lax.broadcasted_iota(jnp.int32, (span, span), 0)
        - lax.broadcasted_iota(jnp.int32, (span, span), 1)
    ).astype(F32)
    causal = gap >= 0.0

    def cols(h):
        return pl.ds(pl.multiple_of(h * width, width), width)

    def within_of(h):
        return jnp.where(causal, jnp.exp(-rates_ref[h] * jnp.where(causal, gap, 0.0)), 0.0)

    def rising_of(h):
        return jnp.exp(-rates_ref[h] * rows)

    def falling_of(h):
        return jnp.exp(-rates_ref[h] * (span - rows))

    def copy(src, dst, send, recv, at, rel, j, target):
        return pltpu.make_async_remote_copy(
            src_ref=src.at[pl.ds(at, CHUNK)],
            dst_ref=dst.at[pl.ds(rel, CHUNK)],
            send_sem=send.at[j],
            recv_sem=recv.at[j],
            device_id={"seq": target},
            device_id_type=MESH,
        )

    def swap(j, back):
        if back:
            return copy(bstate, bpeer, bsend_a, brecv_a, other + j * CHUNK, j * CHUNK, j, mate)
        return copy(state, peer, send_a, recv_a, other + j * CHUNK, j * CHUNK, j, mate)

    def hop(j, back):
        if back:
            return copy(bcout, bcin, bsend_c, brecv_c, j * CHUNK, j * CHUNK, j, seq - 2)
        return copy(cout, cin, send_c, recv_c, j * CHUNK, j * CHUNK, j, seq + 2)

    def hand(j, back):
        if back:
            return copy(bgive, btake, bsend_p, brecv_p, j * CHUNK, j * CHUNK, j, mate)
        return copy(give, take, send_p, recv_p, j * CHUNK, j * CHUNK, j, mate)

    def chain(j, back):
        mine_ref, peer_ref, in_ref, out_ref, give_ref = (
            (bstate, bpeer, bcin, bcout, bgive) if back else (state, peer, cin, cout, give)
        )
        leads = (column == 1) if back else (column == 0)
        has_in = (group < groups - 1) if back else (group > 0)
        has_out = (group > 0) if back else (group < groups - 1)

        @pl.when(has_in)
        def _():
            hop(j, back).wait_recv()

        for i in range(CHUNK):
            rel = j * CHUNK + i
            h = own + rel
            decay = jnp.exp(jnp.full((1, width), -rates_ref[h] * span, F32))
            one = jnp.ones_like(decay)
            zero = jnp.zeros_like(decay)
            lead_decay = jnp.where(leads, decay, one)
            trail_decay = jnp.where(leads, one, decay)
            mine = mine_ref[h]
            theirs = peer_ref[rel]
            carry = in_ref[rel]
            out_ref[rel] = decay * decay * carry + lead_decay * mine + trail_decay * theirs
            give_ref[rel] = lead_decay * carry + jnp.where(leads, one, zero) * mine
            kept = (trail_decay * carry + jnp.where(leads, zero, one) * theirs).astype(BF16)
            if back:
                later_half[rel] = kept
            else:
                prefix_half[h] = kept

        @pl.when(has_out)
        def _():
            hop(j, back).start()

    def make_state(h):
        keys = (k_ref[:, cols(h)].astype(F32) * falling_of(h)).astype(BF16)
        state[h] = dot(keys, v_ref[:, cols(h)], 0, 0)

    def finish_front(h, inner, prefix):
        q = q_ref[:, cols(h)]
        attended = inner + rising_of(h) * dot(q, prefix, 1, 0)
        inverse = lax.rsqrt(jnp.mean(attended * attended, axis=1, keepdims=True) + norm_epsilon)
        unit = attended * inverse
        normed[h] = unit
        weights = gain_ref[pl.ds(h, 1), :] * probe_ref[pl.ds(h, 1), :]
        weighted = unit * weights
        slim[h] = (weights - unit * jnp.mean(weighted, axis=1, keepdims=True)) * inverse
        logit_sum[...] += weighted

    def inner_of(h):
        q = q_ref[:, cols(h)]
        mixed = (dot(q, k_ref[:, cols(h)], 1, 1) * within_of(h)).astype(BF16)
        mix[h] = mixed
        sq[h] = (q.astype(F32) * rising_of(h)).astype(BF16)
        return dot(mixed, v_ref[:, cols(h)], 1, 0)

    def make_first(j, carry):
        for i in range(CHUNK):
            make_state(other + j * CHUNK + i)
        return carry

    flight = min(FLIGHT, chunks)

    def lead_first(j, carry):
        make_first(j, carry)
        swap(j, False).start()
        return carry

    for load in loads[:3]:
        load.wait()
    make_first(0, 0)
    edges = jnp.where(group > 0, 1, 0) + jnp.where(group < groups - 1, 1, 0)
    pl.semaphore_wait(barrier, len(exchanges) + edges)
    swap(0, False).start()
    lax.fori_loop(1, flight, lead_first, 0)
    lax.fori_loop(flight, chunks, make_first, 0)

    def make_own(j):
        for i in range(CHUNK):
            make_state(own + j * CHUNK + i)

    make_own(0)
    for load in loads[3:]:
        load.wait()

    steps = ends_ref.shape[1]
    position = seq * span + lax.broadcasted_iota(jnp.int32, (span, steps), 0)
    segment = jnp.sum(jnp.where(ends_ref[...] < position, 1.0, 0.0), axis=1, keepdims=True)
    step_at = lax.broadcasted_iota(jnp.int32, (span, steps), 1).astype(F32)
    fractions = counts_ref[...].astype(F32) / ROLLOUTS
    targets = jnp.sum(jnp.where(step_at == segment, fractions, 0.0), axis=1, keepdims=True)

    def pace(i, back, after):
        place = (groups - 1 - group) if back else group
        at = i - jnp.minimum(2 * place, chunks - flight)

        @pl.when((at >= 0) & (at < chunks))
        def _():
            chain(at, back)

        @pl.when(i + flight < chunks)
        def _():
            swap(i + flight, back).start()

        @pl.when((i + flight >= chunks) & (i + flight < 2 * chunks))
        def _():
            hand(i + flight - chunks, back).start()

        @pl.when((at >= 0) & (at < chunks))
        def _():
            after(at)

    def own_front(j):
        for i in range(CHUNK):
            h = own + j * CHUNK + i
            finish_front(h, inner_of(h), prefix_half[h])

    def forward(i, carry):
        swap(i, False).wait_recv()
        pace(i, False, own_front)

        @pl.when(i + 1 < chunks)
        def _():
            make_own(i + 1)

        for c in range(CHUNK):
            h = other + i * CHUNK + c
            gk_part[h] = inner_of(h)
        return carry

    lax.fori_loop(0, chunks, forward, 0)

    def forward_rest(j, carry):
        hand(j, False).wait_recv()
        pace(j + chunks, False, own_front)
        for i in range(CHUNK):
            rel = j * CHUNK + i
            h = other + rel
            prefix_half[h] = take[rel].astype(BF16)
            finish_front(h, gk_part[h], prefix_half[h])
        return carry

    lax.fori_loop(0, chunks, forward_rest, 0)

    logits = jnp.sum(logit_sum[...], axis=1, keepdims=True)
    soft = jnp.maximum(logits, 0.0) + jnp.log1p(jnp.exp(-jnp.abs(logits)))
    loss = jnp.sum(soft - targets * logits, axis=0, keepdims=True) / length
    slope = loss_scaling * (jax.nn.sigmoid(logits) - targets) / length
    slope_wide = jnp.broadcast_to(slope, (span, width))
    logit_sum[...] = slope_wide
    sums[0, pl.ds(heads, 8), :] = jnp.broadcast_to(loss, (8, width))

    def make_back(h):
        steep = logit_sum[...]
        grad = (steep * slim[h]).astype(BF16)
        og[h] = grad
        bstate[h] = dot(sq[h], grad, 0, 0)
        sums[0, pl.ds(h, 1), :] = jnp.sum(steep * normed[h], axis=0, keepdims=True)

    def back_first(j, carry):
        for i in range(CHUNK):
            make_back(other + j * CHUNK + i)
        return carry

    def lead_back(j, carry):
        back_first(j, carry)
        swap(j, True).start()
        return carry

    lax.fori_loop(0, flight, lead_back, 0)
    lax.fori_loop(flight, chunks, back_first, 0)

    def back_own(j):
        for i in range(CHUNK):
            make_back(own + j * CHUNK + i)

    back_own(0)

    def back_parts(h):
        grad = og[h]
        k = k_ref[:, cols(h)]
        q = q_ref[:, cols(h)]
        back_mix = (dot(grad, v_ref[:, cols(h)], 1, 1) * within_of(h)).astype(BF16)
        grad_q = dot(back_mix, k, 1, 0) + rising_of(h) * dot(grad, prefix_half[h], 1, 1)
        gq_ref[:, cols(h)] = grad_q.astype(BF16)
        return dot(back_mix, q, 0, 0), dot(mix[h], grad, 0, 0)

    def finish_back(h, grad_k, grad_v, later):
        falling = falling_of(h)
        grad_k = grad_k + falling * dot(v_ref[:, cols(h)], later, 1, 1)
        grad_v = grad_v + falling * dot(k_ref[:, cols(h)], later, 1, 0)
        gk_ref[:, cols(h)] = grad_k.astype(BF16)
        gv_ref[:, cols(h)] = grad_v.astype(BF16)

    def own_back(j):
        for i in range(CHUNK):
            h = own + j * CHUNK + i
            grad_k, grad_v = back_parts(h)
            finish_back(h, grad_k, grad_v, later_half[j * CHUNK + i])

    def backward(i, carry):
        swap(i, True).wait_recv()
        pace(i, True, own_back)

        @pl.when(i + 1 < chunks)
        def _():
            back_own(i + 1)

        for c in range(CHUNK):
            h = other + i * CHUNK + c
            gk_part[h], gv_part[h] = back_parts(h)
        return carry

    lax.fori_loop(0, chunks, backward, 0)

    def total(at):
        axis, partner = exchanges[at]
        return pltpu.make_async_remote_copy(
            src_ref=sums.at[at],
            dst_ref=sums_in.at[at],
            send_sem=send_s.at[at],
            recv_sem=recv_s.at[at],
            device_id={axis: partner},
            device_id_type=MESH,
        )

    def backward_rest(j):
        hand(j, True).wait_recv()
        pace(j + chunks, True, own_back)
        for i in range(CHUNK):
            rel = j * CHUNK + i
            h = other + rel
            finish_back(h, gk_part[h], gv_part[h], btake[rel].astype(BF16))

    def save(j):
        if j == chunks:
            part = pl.ds(pl.multiple_of(own * width, width), half * width)
        else:
            part = pl.ds(
                pl.multiple_of((other + j * CHUNK) * width, width), CHUNK * width
            )
        return [
            pltpu.make_async_copy(source.at[:, part], target.at[:, part], save_sem.at[at, j])
            for at, (source, target) in enumerate(
                ((gq_ref, gq_hbm), (gk_ref, gk_hbm), (gv_ref, gv_hbm))
            )
        ]

    total(0).start()
    for j in range(max(chunks, len(exchanges))):
        if j < chunks:
            backward_rest(j)
            for saved in save(j):
                saved.start()
        if j == chunks - flight:
            for saved in save(chunks):
                saved.start()
        if j < len(exchanges):
            total(j).wait_recv()
            sums[j + 1] = sums[j] + sums_in[j]
            if j + 1 < len(exchanges):
                total(j + 1).start()

    last = len(exchanges)
    summed = sums[last, pl.ds(0, heads), :]
    ggain_ref[...] = summed * probe_ref[...]
    gprobe_ref[...] = summed * gain_ref[...]
    loss_ref[...] = sums[last, pl.ds(heads, 1), pl.ds(0, 1)]

    for j in range(chunks + 1):
        for saved in save(j):
            saved.wait()
    for at in range(len(exchanges)):
        total(at).wait_send()

    def drain(j, carry):
        for back in (False, True):
            swap(j, back).wait_send()
            hand(j, back).wait_send()

        @pl.when(group < groups - 1)
        def _():
            hop(j, False).wait_send()

        @pl.when(group > 0)
        def _():
            hop(j, True).wait_send()

        return carry

    lax.fori_loop(0, chunks, drain, 0)


def store(*refs):
    sources, targets, held, sem_in, sem_out = refs[:6], refs[6:12], refs[12:18], refs[18], refs[19]
    count = len(sources)
    ins = [pltpu.make_async_copy(sources[n], held[n], sem_in.at[n]) for n in range(count)]
    outs = [pltpu.make_async_copy(held[n], targets[n], sem_out.at[n]) for n in range(count)]
    for copy in ins:
        copy.start()
    for n in range(count):
        ins[n].wait()
        outs[n].start()
    for copy in outs:
        copy.wait()


def solution(mesh):
    n_dp = mesh.shape["dp"]
    n_seq = mesh.shape["seq"]
    exchanges = len(bits_of(n_dp)) + len(bits_of(n_seq))

    def on_device(
        queries, key_rows, value_rows, decay_rates, norm_gain, reward_probe, step_ends, step_counts
    ):
        heads = decay_rates.shape[0]
        _, span, features = queries.shape
        width = features // heads
        half = heads // 2
        chunks = half // CHUNK
        hbm = pl.BlockSpec(memory_space=pltpu.HBM)
        vmem = pl.BlockSpec(memory_space=pltpu.VMEM)
        rows = jax.ShapeDtypeStruct((span, features), BF16)
        table = jax.ShapeDtypeStruct((heads, width), F32)

        def scan_buffers():
            return [pltpu.VMEM((heads, width, width), F32)] + [
                pltpu.VMEM((half, width, width), F32)
            ] * 5

        results = pl.pallas_call(
            functools.partial(layer, n_dp, n_seq),
            out_shape=(jax.ShapeDtypeStruct((1, 1), F32), rows, rows, rows, table, table),
            in_specs=[hbm] * 8,
            out_specs=(vmem, hbm, hbm, hbm, vmem, vmem),
            scratch_shapes=[pltpu.VMEM((span, features), BF16)] * 3
            + [
                pltpu.SemaphoreType.DMA((3, chunks + 1)),
                pltpu.SMEM((heads,), F32),
                pltpu.VMEM((span, features), BF16),
                pltpu.VMEM((span, features), BF16),
                pltpu.VMEM((span, features), BF16),
                pltpu.VMEM((heads, width), F32),
                pltpu.VMEM((heads, width), F32),
                pltpu.VMEM(step_ends.shape, jnp.int32),
                pltpu.VMEM(step_counts.shape, jnp.int32),
                pltpu.SemaphoreType.DMA((8,)),
            ]
            + scan_buffers()
            + scan_buffers()
            + [
                pltpu.VMEM((heads, width, width), BF16),
                pltpu.VMEM((half, width, width), BF16),
                pltpu.VMEM((heads, span, span), BF16),
                pltpu.VMEM((heads, span, width), F32),
                pltpu.VMEM((heads, span, width), F32),
                pltpu.VMEM((heads, span, width), F32),
                pltpu.VMEM((heads, span, width), F32),
                pltpu.VMEM((heads, span, width), BF16),
                pltpu.VMEM((heads, span, width), BF16),
                pltpu.VMEM((span, width), F32),
                pltpu.VMEM((exchanges + 1, heads + 8, width), F32),
                pltpu.VMEM((exchanges, heads + 8, width), F32),
            ]
            + [pltpu.SemaphoreType.DMA((chunks,))] * 12
            + [pltpu.SemaphoreType.DMA((exchanges,))] * 2,
            compiler_params=pltpu.CompilerParams(
                collective_id=0, has_side_effects=True, vmem_limit_bytes=60 * 1024 * 1024
            ),
            cost_estimate=pl.CostEstimate(
                flops=28 * heads * span * width * width,
                bytes_accessed=12 * span * features,
                transcendentals=6 * heads * span * width,
            ),
        )(
            decay_rates,
            queries[0],
            key_rows[0],
            value_rows[0],
            norm_gain.reshape(heads, width),
            reward_probe.reshape(heads, width),
            step_ends,
            step_counts,
        )
        loss, gq, gk, gv, ggain, gprobe = pl.pallas_call(
            store,
            out_shape=tuple(jax.ShapeDtypeStruct(a.shape, a.dtype) for a in results),
            in_specs=[hbm] * 6,
            out_specs=(hbm,) * 6,
            scratch_shapes=[pltpu.VMEM(a.shape, a.dtype) for a in results]
            + [pltpu.SemaphoreType.DMA((6,))] * 2,
            compiler_params=pltpu.CompilerParams(vmem_limit_bytes=60 * 1024 * 1024),
        )(*results)
        return (
            loss.reshape(()),
            gq[None],
            gk[None],
            gv[None],
            ggain.reshape(features),
            gprobe.reshape(features),
        )

    rows = P("dp", "seq", None)
    return jax.shard_map(
        on_device,
        mesh=mesh,
        in_specs=(rows, rows, rows, P(), P(), P(), P("dp", None), P("dp", None)),
        out_specs=(P(), rows, rows, rows, P(), P()),
        check_vma=False,
    )
```
